32 devices in a mesh: grp: 2 (over y), col: 8 (over z, x), row: 2 (over core).
Axes of the slice: x: 2, y: 2, z: 4, core: 2. Of those that a mesh axis runs over, the one named last changes fastest.
Arguments:
- genotypes: float32 [6, 12288, 256], P(None, ('grp', 'col', 'row')), parts along dimension 1, may hold values from -1 to 2, as said below
- prior_slab: float32 [1536, 6144], P(('grp', 'row'), 'col'), parts along dimension 0, may hold values from -6 to 6
Outputs:
- updated_slab: float32 [1536, 6144], P(('grp', 'row'), 'col'), parts along dimension 0
The draws below stay inside these ranges and needn't reach their ends.
There are 2 independent parts, one for each index of `grp`. The reference program is written for one: setup_inputs(seed, part) draws one part's arguments, and reference() takes and returns one part's arrays. A program takes and returns all parts, laid end to end along the dimension named above; each array names one. Nothing has to cross between parts.
Inputs may be any that keep to these rules, and one draw needn't show every extreme that they name: `genotypes`: each variant has its own allele frequency, which drifts with the sample index; about one call in twenty is missing (value -1), and in every block one variant has no called sample at all.
All inputs are finite; a program needn't handle non-finite values.
Results may differ from the reference program's by a relative error of at most 0.0003.
Values sent between devices are 32-bit elements; how exact they have to be, the bound alone decides.
A program may use at most 64 MiB of HBM per device.

```python
import jax
import jax.numpy as jnp
from jax import lax

V = 256
BLOCKS = 6
SAMPLES = 6144
ROWS = 768


def draw_genotypes(key, part):
    key = jax.random.fold_in(key, 7)
    freq_key, first_key, second_key, miss_key, dead_key, noise_key = jax.random.split(key, 6)
    thousandths = jax.random.randint(freq_key, (BLOCKS, 1, V), 2, 334)
    sample_index = jnp.arange(SAMPLES, dtype=jnp.int32)[None, :, None]
    threshold = thousandths * (SAMPLES + 2 * sample_index) // SAMPLES
    first_allele = (jax.random.randint(first_key, (BLOCKS, SAMPLES, V), 0, 1000) < threshold).astype(jnp.int32)
    second_allele = (jax.random.randint(second_key, (BLOCKS, SAMPLES, V), 0, 1000) < threshold).astype(jnp.int32)
    missing = jax.random.randint(miss_key, (BLOCKS, SAMPLES, V), 0, 20) == 0
    dead_variant = jax.random.randint(dead_key, (BLOCKS, 1, 1), 0, V)
    variant_index = jnp.arange(V, dtype=jnp.int32)[None, None, :]
    missing = jnp.logical_or(missing, variant_index == dead_variant)
    hard_call = (first_allele + second_allele).astype(jnp.float32)
    noise = jax.random.uniform(noise_key, (BLOCKS, SAMPLES, V), jnp.float32, -0.3, 0.3)
    value = jnp.abs(hard_call + noise)
    value = 2.0 - jnp.abs(2.0 - value)
    return jnp.where(missing, -1.0, value).astype(jnp.float32)


def steps_of(key, extent, cuts, smallest, largest):
    level = 1.0
    for position, parts in cuts:
        steps = jax.random.uniform(jax.random.fold_in(jax.random.fold_in(key, 6), position), (parts,), jnp.float32, smallest / len(cuts), largest / len(cuts))
        level = level * jnp.repeat(jnp.exp(steps), extent[position] // parts).reshape((-1,) + (1,) * (len(extent) - 1 - position))
    return level


def scatter_about(own_key, shape, scale, most, cuts=(), kind=jnp.bfloat16):
    drawn = scale * jax.random.normal(own_key, shape, jnp.float32)
    if cuts:
        drawn = drawn * steps_of(own_key, shape, cuts, -0.22, 0.18)
    return jnp.clip(drawn, -most, most).astype(kind)


def setup_inputs(seed: int = 0, part: int = 0) -> dict:
    arg_keys = jax.random.split(jax.random.key(seed), 3)
    own_keys = jax.random.split(jax.random.fold_in(arg_keys[2], part), 3)
    genotypes = draw_genotypes(jax.random.fold_in(jax.random.fold_in(arg_keys[2], part), 71), part)
    prior_slab = scatter_about(own_keys[1], (ROWS, SAMPLES), 1.0, 6.0, ((0, 2), (1, 8)), jnp.float32)
    return dict(genotypes=genotypes, prior_slab=prior_slab)


def reference(genotypes, prior_slab):
    called = genotypes >= 0
    dosage = jnp.where(called, genotypes, 0.0).astype(jnp.float32)
    allele_sum = lax.optimization_barrier(jnp.sum(dosage, axis=1))
    square_sum = lax.optimization_barrier(jnp.sum(dosage * dosage, axis=1))
    counts = lax.optimization_barrier(jnp.sum(called.astype(jnp.float32), axis=1))
    counts = jnp.maximum(counts, 1.0)
    center = allele_sum / counts
    spread = jnp.sqrt(jnp.maximum(square_sum / counts - center * center, 0.05))
    zscore = jnp.where(called, (dosage - center[:, None, :]) / spread[:, None, :], 0.0)
    row_part = zscore[:, :ROWS, :]
    factor = 1.0 / jnp.sqrt(jnp.float32(BLOCKS * V))
    total = jnp.einsum('kiv,kjv->ij', row_part, zscore, precision=lax.Precision.HIGHEST)
    return prior_slab + total * factor
```

```python
import functools
import math

import jax
import jax.numpy as jnp
from jax import lax
from jax.experimental import pallas as pl
from jax.experimental.pallas import tpu as pltpu
from jax.sharding import PartitionSpec as P

MESH = pl.DeviceIdType.MESH
PIECES = 4
SKEW = 2
WINDOW = 3


def grid_of(count):
    fast = 2 ** (int(math.log2(count)) // 2)
    return count // fast, fast


def split(values):
    high = values.astype(jnp.bfloat16)
    return high, (values - high.astype(jnp.float32)).astype(jnp.bfloat16)


def kernel(slow_n, fast_n, calls_hbm, prior_hbm, out_ref, own, other, rows, high_t, low_t,
           sums, sums_in, scaling, local_sem, pair_send, pair_recv, stat_send, stat_recv,
           piece_send, piece_recv):
    blocks, samples, variants = own.shape
    stages = sums_in.shape[0]
    piece = samples // PIECES
    pieces = blocks * PIECES
    depth_max = max(slow_n + fast_n - 2, fast_n + 1, slow_n + 1)

    grp, col, row = lax.axis_index("grp"), lax.axis_index("col"), lax.axis_index("row")
    z, x = col // fast_n, col % fast_n
    first, second = jnp.where(row == 0, z, x), jnp.where(row == 0, x, z)
    first_n = jnp.where(row == 0, slow_n, fast_n)
    second_n = jnp.where(row == 0, fast_n, slow_n)

    def device(a, b):
        return (grp, jnp.where(row == 0, a * fast_n + b, b * fast_n + a), row)

    is_root = col == 0
    on_edge = jnp.logical_and(first == 0, second > 0)
    on_spine = second == 0
    depth = jnp.where(on_edge, second + 2, first + second)
    parent = device(
        jnp.where(on_edge, 1, jnp.where(on_spine, jnp.maximum(first - 1, 0), first)),
        jnp.where(on_edge, second, jnp.where(on_spine, 0, second - 1)),
    )
    has_a = jnp.logical_and(
        jnp.logical_not(on_edge),
        jnp.where(on_spine, first + 1 < first_n, second + 1 < second_n),
    )
    child_a = device(
        jnp.where(on_spine, jnp.minimum(first + 1, first_n - 1), first),
        jnp.where(on_spine, 0, jnp.minimum(second + 1, second_n - 1)),
    )
    has_b = jnp.where(on_spine, first >= 1, first == 1)
    child_b = device(jnp.where(on_spine, first, 0), jnp.where(on_spine, 1, second))

    pair = (grp, col, 1 - row)

    def partner(stage):
        if stage == 0:
            return pair
        bit = 2 ** (stage - 1)
        return (grp, col + bit - 2 * bit * ((col // bit) % 2), row)

    own_copy = pltpu.make_async_copy(calls_hbm, own, local_sem.at[0])
    own_copy.start()
    prior_copy = pltpu.make_async_copy(prior_hbm, out_ref, local_sem.at[1])
    prior_copy.start()
    root_copy = pltpu.make_async_copy(calls_hbm, rows, local_sem.at[2])

    barrier = pltpu.get_barrier_semaphore()
    for stage in range(stages):
        pl.semaphore_signal(barrier, inc=1, device_id=partner(stage), device_id_type=MESH)

    @pl.when(jnp.logical_not(is_root))
    def _():
        pl.semaphore_signal(barrier, inc=1, device_id=parent, device_id_type=MESH)

    @pl.when(has_a)
    def _():
        pl.semaphore_signal(barrier, inc=1, device_id=child_a, device_id_type=MESH)

    @pl.when(has_b)
    def _():
        pl.semaphore_signal(barrier, inc=1, device_id=child_b, device_id_type=MESH)

    greeted = (stages + jnp.where(is_root, 0, 1) + jnp.where(has_a, 1, 0) + jnp.where(has_b, 1, 0))
    pl.semaphore_wait(barrier, greeted)

    def part(ref, c):
        return ref.at[c // PIECES, pl.ds(pl.multiple_of((c % PIECES) * piece, piece), piece)]

    def from_root(c):
        return pltpu.make_async_remote_copy(
            src_ref=part(calls_hbm, c), dst_ref=part(rows, c), send_sem=piece_send.at[0, c],
            recv_sem=piece_recv.at[c], device_id=child_a, device_id_type=MESH)

    def forward(c, which, target):
        return pltpu.make_async_remote_copy(
            src_ref=part(rows, c), dst_ref=part(rows, c), send_sem=piece_send.at[which, c],
            recv_sem=piece_recv.at[c], device_id=target, device_id_type=MESH)

    def pair_copy(k):
        return pltpu.make_async_remote_copy(
            src_ref=calls_hbm.at[k], dst_ref=other.at[k], send_sem=pair_send.at[k],
            recv_sem=pair_recv.at[k], device_id=pair, device_id_type=MESH)

    def stat_copy(stage):
        return pltpu.make_async_remote_copy(
            src_ref=sums.at[stage], dst_ref=sums_in.at[stage], send_sem=stat_send.at[stage],
            recv_sem=stat_recv.at[stage], device_id=partner(stage), device_id_type=MESH)

    @pl.when(is_root)
    def _():
        for c in range(min(WINDOW, pieces)):
            from_root(c).start()
        root_copy.start()

    own_copy.wait()

    def local_sums(k, carry):
        values = own[k]
        called = values >= 0
        dosage = jnp.where(called, values, 0.0)
        sums[0, 0, pl.ds(k, 1), :] = jnp.sum(dosage, axis=0, keepdims=True)
        sums[0, 1, pl.ds(k, 1), :] = jnp.sum(dosage * dosage, axis=0, keepdims=True)
        sums[0, 2, pl.ds(k, 1), :] = jnp.sum(jnp.where(called, 1.0, 0.0), axis=0, keepdims=True)
        return carry

    lax.fori_loop(0, blocks, local_sums, 0)
    stat_copy(0).start()

    @pl.when(is_root)
    def _():
        root_copy.wait()

    prior_copy.wait()

    stat_slots = [1 + 2 * stage for stage in range(stages)]
    prep_slot = stat_slots[-1] + 1
    lag = max(SKEW * (depth_max - 1), prep_slot + 1 - (PIECES - 1))
    slots = lag + pieces
    factor = 1.0 / math.sqrt(blocks * variants)

    def standardize(values, k):
        center, scale = scaling[0, pl.ds(k, 1), :], scaling[1, pl.ds(k, 1), :]
        return jnp.where(values >= 0, (values - center) * scale, 0.0)

    def slot(s, carry):
        c = s - SKEW * (depth - 1)
        in_range = jnp.logical_and(c >= 0, c < pieces)

        @pl.when(jnp.logical_and(in_range, jnp.logical_not(is_root)))
        def _():
            forward(c, 0, parent).wait_recv()

            @pl.when(has_a)
            def _():
                forward(c, 0, child_a).start()

            @pl.when(has_b)
            def _():
                forward(c, 1, child_b).start()

        @pl.when(jnp.logical_and(is_root, s < pieces))
        def _():
            from_root(s).wait_send()

            @pl.when(s + WINDOW < pieces)
            def _():
                from_root(s + WINDOW).start()

        for stage, at in enumerate(stat_slots):
            @pl.when(s == at)
            def _():
                stat_copy(stage).wait_recv()
                total = sums[stage] + sums_in[stage]
                sums[stage + 1] = total
                if stage + 1 < stages:
                    stat_copy(stage + 1).start()
                else:
                    counts = jnp.maximum(total[2], 1.0)
                    center = total[0] / counts
                    spread = jnp.sqrt(jnp.maximum(total[1] / counts - center * center, 0.05))
                    scaling[0] = center
                    scaling[1] = 1.0 / spread

        @pl.when(jnp.logical_and(s >= 1, s < 1 + blocks))
        def _():
            pair_copy(s - 1).start()

        @pl.when(jnp.logical_and(s >= prep_slot, s < prep_slot + blocks))
        def _():
            k = s - prep_slot
            pair_copy(k).wait_recv()
            for held, place in ((own, row), (other, 1 - row)):
                for at in range(0, samples, 128):
                    scores = standardize(held[k, at:at + 128, :], k) * factor
                    high, low = split(scores.T)
                    lanes = pl.ds(pl.multiple_of(place * samples + at, 128), 128)
                    high_t[k, :, lanes] = high
                    low_t[k, :, lanes] = low

        @pl.when(jnp.logical_and(s >= lag + PIECES - 1, (s - lag) % PIECES == PIECES - 1))
        def _():
            k = (s - lag) // PIECES
            high, low = split(standardize(rows[k], k))

            def tile(n, carry):
                lanes = pl.ds(pl.multiple_of(n * 256, 256), 256)
                right_high, right_low = high_t[k, :, lanes], low_t[k, :, lanes]
                dot = functools.partial(jnp.dot, preferred_element_type=jnp.float32)
                out_ref[:, lanes] += (
                    dot(high, right_high) + (dot(low, right_high) + dot(high, right_low)))
                return carry

            lax.fori_loop(0, out_ref.shape[1] // 256, tile, 0)

        return carry

    lax.fori_loop(0, slots, slot, 0)

    for stage in range(stages):
        stat_copy(stage).wait_send()

    def drain_pair(k, carry):
        pair_copy(k).wait_send()
        return carry

    lax.fori_loop(0, blocks, drain_pair, 0)

    def drain(c, carry):
        @pl.when(jnp.logical_and(has_a, jnp.logical_not(is_root)))
        def _():
            forward(c, 0, child_a).wait_send()

        @pl.when(has_b)
        def _():
            forward(c, 1, child_b).wait_send()

        return carry

    lax.fori_loop(0, pieces, drain, 0)


def per_device(slow_n, fast_n, genotypes, prior_slab):
    blocks, samples, variants = genotypes.shape
    height, width = prior_slab.shape
    stages = 1 + int(math.log2(slow_n * fast_n))
    pieces = blocks * PIECES
    return pl.pallas_call(
        functools.partial(kernel, slow_n, fast_n),
        out_shape=jax.ShapeDtypeStruct((height, width), jnp.float32),
        in_specs=[pl.BlockSpec(memory_space=pl.ANY)] * 2,
        out_specs=pl.BlockSpec(memory_space=pltpu.VMEM),
        scratch_shapes=[
            pltpu.VMEM((blocks, samples, variants), jnp.float32),
            pltpu.VMEM((blocks, samples, variants), jnp.float32),
            pltpu.VMEM((blocks, samples, variants), jnp.float32),
            pltpu.VMEM((blocks, variants, width), jnp.bfloat16),
            pltpu.VMEM((blocks, variants, width), jnp.bfloat16),
            pltpu.VMEM((stages + 1, 3, blocks, variants), jnp.float32),
            pltpu.VMEM((stages, 3, blocks, variants), jnp.float32),
            pltpu.VMEM((2, blocks, variants), jnp.float32),
            pltpu.SemaphoreType.DMA((3,)),
            pltpu.SemaphoreType.DMA((blocks,)),
            pltpu.SemaphoreType.DMA((blocks,)),
            pltpu.SemaphoreType.DMA((stages,)),
            pltpu.SemaphoreType.DMA((stages,)),
            pltpu.SemaphoreType.DMA((2, pieces)),
            pltpu.SemaphoreType.DMA((pieces,)),
        ],
        compiler_params=pltpu.CompilerParams(
            collective_id=0, has_side_effects=True, vmem_limit_bytes=48 * 2**20),
        cost_estimate=pl.CostEstimate(
            flops=6 * height * width * blocks * variants,
            bytes_accessed=4 * (2 * blocks * samples * variants + 2 * height * width),
            transcendentals=0),
    )(genotypes, prior_slab)


def solution(mesh):
    slow_n, fast_n = grid_of(mesh.shape["col"])
    placed = (P(None, ("grp", "col", "row"), None), P(("grp", "row"), "col"))
    return jax.shard_map(
        functools.partial(per_device, slow_n, fast_n), mesh=mesh, in_specs=placed,
        out_specs=P(("grp", "row"), "col"), check_vma=False
    )
```

```python
import functools
import math

import jax
import jax.numpy as jnp
from jax import lax
from jax.experimental import pallas as pl
from jax.experimental.pallas import tpu as pltpu
from jax.sharding import PartitionSpec as P

MESH = pl.DeviceIdType.MESH
PIECES = 8
WINDOW = 8
GATHERED = 7
TOTALLED = 10
VMEM_MIB = 52


def grid_of(count):
    fast = 2 ** (int(math.log2(count)) // 2)
    return count // fast, fast


def split(values):
    high = values.astype(jnp.bfloat16)
    return high, (values - high.astype(jnp.float32)).astype(jnp.bfloat16)


def kernel(slow_n, fast_n, calls_hbm, out_ref, own, other, rows, high, low, row_high, row_low,
           sums, gathered, joined, joined_in, totals, scaling, local_sem, pair_send, pair_recv,
           sums_send, sums_recv, joined_sem, totals_send, totals_recv, piece_send, piece_recv):
    blocks, samples, variants = own.shape
    columns = gathered.shape[0]
    piece = samples // PIECES
    pieces = blocks * PIECES
    arrival = TOTALLED + WINDOW

    grp, col, row = lax.axis_index("grp"), lax.axis_index("col"), lax.axis_index("row")
    z, x = col // fast_n, col % fast_n
    first, second = jnp.where(row == 0, z, x), jnp.where(row == 0, x, z)
    first_n = jnp.where(row == 0, slow_n, fast_n)
    second_n = jnp.where(row == 0, fast_n, slow_n)

    def device(a, b):
        return (grp, jnp.where(row == 0, a * fast_n + b, b * fast_n + a), row)

    is_root = col == 0
    on_edge = jnp.logical_and(first == 0, second > 0)
    on_spine = second == 0
    parent = device(
        jnp.where(on_edge, 1, jnp.where(on_spine, jnp.maximum(first - 1, 0), first)),
        jnp.where(on_edge, second, jnp.where(on_spine, 0, second - 1)),
    )
    has_a = jnp.logical_and(
        jnp.logical_not(on_edge),
        jnp.where(on_spine, first + 1 < first_n, second + 1 < second_n),
    )
    child_a = device(
        jnp.where(on_spine, jnp.minimum(first + 1, first_n - 1), first),
        jnp.where(on_spine, 0, jnp.minimum(second + 1, second_n - 1)),
    )
    has_b = jnp.where(on_spine, first >= 1, first == 1)
    child_b = device(jnp.where(on_spine, first, 0), jnp.where(on_spine, 1, second))

    pair = (grp, col, 1 - row)

    root = (grp, 0, row)

    own_copy = pltpu.make_async_copy(calls_hbm, own, local_sem.at[0])
    own_copy.start()
    root_copy = pltpu.make_async_copy(calls_hbm, rows, local_sem.at[1])

    barrier = pltpu.get_barrier_semaphore()
    pl.semaphore_signal(barrier, inc=1, device_id=pair, device_id_type=MESH)

    @pl.when(jnp.logical_not(is_root))
    def _():
        pl.semaphore_signal(barrier, inc=1, device_id=parent, device_id_type=MESH)

    @pl.when(is_root)
    def _():
        def greet(j, carry):
            pl.semaphore_signal(barrier, inc=1, device_id=(grp, j, row), device_id_type=MESH)
            return carry

        lax.fori_loop(1, columns, greet, 0)

    pl.semaphore_wait(
        barrier,
        1 + jnp.where(is_root, 0, 1) + jnp.where(has_a, 1, 0) + jnp.where(has_b, 1, 0))

    def part(ref, c):
        return ref.at[c // PIECES, pl.ds(pl.multiple_of((c % PIECES) * piece, piece), piece)]

    def from_root(c):
        return pltpu.make_async_remote_copy(
            src_ref=part(calls_hbm, c), dst_ref=part(rows, c), send_sem=piece_send.at[0, c],
            recv_sem=piece_recv.at[c], device_id=child_a, device_id_type=MESH)

    def forward(c, which, target):
        return pltpu.make_async_remote_copy(
            src_ref=part(rows, c), dst_ref=part(rows, c), send_sem=piece_send.at[which, c],
            recv_sem=piece_recv.at[c], device_id=target, device_id_type=MESH)

    def pair_copy(k):
        return pltpu.make_async_remote_copy(
            src_ref=calls_hbm.at[k], dst_ref=other.at[k], send_sem=pair_send.at[k],
            recv_sem=pair_recv.at[k], device_id=pair, device_id_type=MESH)

    def sums_copy(j):
        return pltpu.make_async_remote_copy(
            src_ref=sums, dst_ref=gathered.at[j], send_sem=sums_send, recv_sem=sums_recv.at[j],
            device_id=root, device_id_type=MESH)

    joined_copy = pltpu.make_async_remote_copy(
        src_ref=joined, dst_ref=joined_in, send_sem=joined_sem.at[0], recv_sem=joined_sem.at[1],
        device_id=pair, device_id_type=MESH)

    def totals_copy(which, target):
        return pltpu.make_async_remote_copy(
            src_ref=totals, dst_ref=totals, send_sem=totals_send.at[which], recv_sem=totals_recv,
            device_id=target, device_id_type=MESH)

    @pl.when(is_root)
    def _():
        for c in range(min(WINDOW, pieces)):
            from_root(c).start()
        root_copy.start()

    own_copy.wait()

    def local_sums(k, carry):
        values = own[k]
        called = values >= 0
        dosage = jnp.where(called, values, 0.0)
        sums[0, pl.ds(k, 1), :] = jnp.sum(dosage, axis=0, keepdims=True)
        sums[1, pl.ds(k, 1), :] = jnp.sum(dosage * dosage, axis=0, keepdims=True)
        sums[2, pl.ds(k, 1), :] = jnp.sum(jnp.where(called, 1.0, 0.0), axis=0, keepdims=True)
        return carry

    lax.fori_loop(0, blocks, local_sums, 0)

    @pl.when(jnp.logical_not(is_root))
    def _():
        sums_copy(col).start()

    @pl.when(is_root)
    def _():
        root_copy.wait()

    out_ref[...] = jnp.zeros_like(out_ref)
    factor = 1.0 / math.sqrt(blocks * variants)

    def standardize(values, k):
        center, scale = scaling[0, pl.ds(k, 1), :], scaling[1, pl.ds(k, 1), :]
        return jnp.where(values >= 0, (values - center) * scale, 0.0)

    def prepare_column(k):
        for held, place in ((own, row), (other, 1 - row)):
            first_part, second_part = split(standardize(held[k], k) * factor)
            spot = pl.ds(pl.multiple_of(place * samples, samples), samples)
            high[k, spot, :] = first_part
            low[k, spot, :] = second_part

    def prepare_row(c):
        k = c // PIECES
        spot = pl.ds(pl.multiple_of((c % PIECES) * piece, piece), piece)
        first_part, second_part = split(standardize(rows[k, spot, :], k))
        row_high[k, spot, :] = first_part
        row_low[k, spot, :] = second_part

    def product(left, right):
        return lax.dot_general(
            left, right, (((1,), (1,)), ((), ())), preferred_element_type=jnp.float32)

    def multiply(k, begin, end):
        left_high, left_low = row_high[k], row_low[k]
        right_high, right_low = high[k, begin:end, :], low[k, begin:end, :]
        out_ref[:, begin:end] += (
            product(left_high, right_high)
            + (product(left_low, right_high) + product(left_high, right_low)))

    width = out_ref.shape[1]

    def step(c, carry):
        @pl.when(jnp.logical_not(is_root))
        def _():
            forward(c, 0, parent).wait_recv()

            @pl.when(has_a)
            def _():
                forward(c, 0, child_a).start()

            @pl.when(has_b)
            def _():
                forward(c, 1, child_b).start()

            @pl.when(c == arrival)
            def _():
                totals_copy(0, parent).wait_recv()

                @pl.when(has_a)
                def _():
                    totals_copy(0, child_a).start()

                @pl.when(has_b)
                def _():
                    totals_copy(1, child_b).start()

        @pl.when(is_root)
        def _():
            from_root(c).wait_send()

            @pl.when(c + WINDOW < pieces)
            def _():
                from_root(c + WINDOW).start()

            @pl.when(c == GATHERED)
            def _():
                joined[...] = sums[...]

                def add(j, carry):
                    sums_copy(j).wait_recv()
                    joined[...] += gathered[j]
                    return carry

                lax.fori_loop(1, columns, add, 0)
                joined_copy.start()

            @pl.when(c == TOTALLED)
            def _():
                joined_copy.wait_recv()
                totals[...] = joined[...] + joined_in[...]
                totals_copy(0, child_a).start()

        @pl.when(c == arrival)
        def _():
            counts = jnp.maximum(totals[2], 1.0)
            center = totals[0] / counts
            spread = jnp.sqrt(jnp.maximum(totals[1] / counts - center * center, 0.05))
            scaling[0] = center
            scaling[1] = 1.0 / spread

        @pl.when(jnp.logical_and(c >= 1, c < 1 + blocks))
        def _():
            pair_copy(c - 1).start()

        since = c - arrival - 1

        @pl.when(jnp.logical_and(since >= 0, since < blocks))
        def _():
            pair_copy(since).wait_recv()
            prepare_column(since)

        for j in range(2):
            @pl.when(jnp.logical_and(since >= 0, 2 * since + j <= c))
            def _():
                prepare_row(2 * since + j)

        @pl.when(jnp.logical_and(since >= 0, c // 2 < since))
        def _():
            prepare_row(c)

        late = arrival + PIECES // 2
        for half in range(2):
            at = c - half
            caught = at // PIECES
            held = (at - late) // (PIECES // 2)
            on_time = jnp.logical_and(
                at % PIECES == PIECES - 1, at >= late + (PIECES // 2) * caught)
            was_held = jnp.logical_and(
                jnp.logical_and(at >= late, (at - late) % (PIECES // 2) == 0),
                at > PIECES * held + PIECES - 1)

            @pl.when(jnp.logical_and(jnp.logical_or(on_time, was_held), at < pieces - 1))
            def _():
                multiply(jnp.where(on_time, caught, held), half * width // 2,
                         (half + 1) * width // 2)

        return carry

    lax.fori_loop(0, pieces, step, 0)
    multiply(blocks - 1, 0, width)

    @pl.when(is_root)
    def _():
        joined_copy.wait_send()
        totals_copy(0, child_a).wait_send()

    @pl.when(jnp.logical_not(is_root))
    def _():
        sums_copy(col).wait_send()

        @pl.when(has_a)
        def _():
            totals_copy(0, child_a).wait_send()

        @pl.when(has_b)
        def _():
            totals_copy(1, child_b).wait_send()

    def drain_pair(k, carry):
        pair_copy(k).wait_send()
        return carry

    lax.fori_loop(0, blocks, drain_pair, 0)

    def drain(c, carry):
        @pl.when(jnp.logical_and(has_a, jnp.logical_not(is_root)))
        def _():
            forward(c, 0, child_a).wait_send()

        @pl.when(has_b)
        def _():
            forward(c, 1, child_b).wait_send()

        return carry

    lax.fori_loop(0, pieces, drain, 0)


def per_device(slow_n, fast_n, genotypes, prior_slab):
    blocks, samples, variants = genotypes.shape
    height, width = prior_slab.shape
    columns = slow_n * fast_n
    pieces = blocks * PIECES
    calls = pltpu.VMEM((blocks, samples, variants), jnp.float32)
    column_part = pltpu.VMEM((blocks, width, variants), jnp.bfloat16)
    row_part = pltpu.VMEM((blocks, samples, variants), jnp.bfloat16)
    sums = pltpu.VMEM((3, blocks, variants), jnp.float32)
    accumulated = pl.pallas_call(
        functools.partial(kernel, slow_n, fast_n),
        out_shape=jax.ShapeDtypeStruct((height, width), jnp.float32),
        in_specs=[pl.BlockSpec(memory_space=pl.ANY)],
        out_specs=pl.BlockSpec(memory_space=pltpu.VMEM),
        scratch_shapes=[
            calls, calls, calls, column_part, column_part, row_part, row_part,
            sums, pltpu.VMEM((columns, 3, blocks, variants), jnp.float32), sums, sums, sums,
            pltpu.VMEM((2, blocks, variants), jnp.float32),
            pltpu.SemaphoreType.DMA((2,)),
            pltpu.SemaphoreType.DMA((blocks,)),
            pltpu.SemaphoreType.DMA((blocks,)),
            pltpu.SemaphoreType.DMA,
            pltpu.SemaphoreType.DMA((columns,)),
            pltpu.SemaphoreType.DMA((2,)),
            pltpu.SemaphoreType.DMA((2,)),
            pltpu.SemaphoreType.DMA,
            pltpu.SemaphoreType.DMA((2, pieces)),
            pltpu.SemaphoreType.DMA((pieces,)),
        ],
        compiler_params=pltpu.CompilerParams(
            collective_id=0, has_side_effects=True, vmem_limit_bytes=VMEM_MIB * 2**20),
        cost_estimate=pl.CostEstimate(
            flops=6 * height * width * blocks * variants,
            bytes_accessed=4 * (blocks * samples * variants + height * width),
            transcendentals=0),
    )(genotypes)
    return prior_slab + accumulated


def solution(mesh):
    slow_n, fast_n = grid_of(mesh.shape["col"])
    placed = (P(None, ("grp", "col", "row"), None), P(("grp", "row"), "col"))
    return jax.shard_map(
        functools.partial(per_device, slow_n, fast_n), mesh=mesh, in_specs=placed,
        out_specs=P(("grp", "row"), "col"), check_vma=False
    )
```

```python
import functools
import math

import jax
import jax.numpy as jnp
from jax import lax
from jax.experimental import pallas as pl
from jax.experimental.pallas import tpu as pltpu
from jax.sharding import PartitionSpec as P

MESH = pl.DeviceIdType.MESH
PIECES = 8
LATE = 3
GATHERED = 7
TOTALLED = 10
VMEM_MIB = 52


def grid_of(count):
    fast = 2 ** (int(math.log2(count)) // 2)
    return count // fast, fast


def split(values):
    high = values.astype(jnp.bfloat16)
    return high, (values - high.astype(jnp.float32)).astype(jnp.bfloat16)


def kernel(slow_n, fast_n, calls_hbm, out_ref, own, other, rows, high, low, row_high, row_low,
           sums, gathered, joined, joined_in, totals, scaling, local_sem, pair_send, pair_recv,
           sums_send, sums_recv, joined_sem, totals_send, totals_recv, root_send,
           piece_send, piece_recv):
    blocks, samples, variants = own.shape
    columns = gathered.shape[0]
    piece = samples // PIECES
    pieces = blocks * PIECES
    arrival = TOTALLED + PIECES

    grp, col, row = lax.axis_index("grp"), lax.axis_index("col"), lax.axis_index("row")
    z, x = lax.div(col, fast_n), lax.rem(col, fast_n)
    first, second = jnp.where(row == 0, z, x), jnp.where(row == 0, x, z)
    first_n = jnp.where(row == 0, slow_n, fast_n)
    second_n = jnp.where(row == 0, fast_n, slow_n)

    def device(a, b):
        return (grp, jnp.where(row == 0, a * fast_n + b, b * fast_n + a), row)

    is_root = col == 0
    on_edge = jnp.logical_and(first == 0, second > 0)
    on_spine = second == 0
    parent = device(
        jnp.where(on_edge, 1, jnp.where(on_spine, jnp.maximum(first - 1, 0), first)),
        jnp.where(on_edge, second, jnp.where(on_spine, 0, second - 1)),
    )
    has_a = jnp.logical_and(
        jnp.logical_not(on_edge),
        jnp.where(on_spine, first + 1 < first_n, second + 1 < second_n),
    )
    child_a = device(
        jnp.where(on_spine, jnp.minimum(first + 1, first_n - 1), first),
        jnp.where(on_spine, 0, jnp.minimum(second + 1, second_n - 1)),
    )
    has_b = jnp.where(on_spine, first >= 1, first == 1)
    child_b = device(jnp.where(on_spine, first, 0), jnp.where(on_spine, 1, second))

    pair = (grp, col, 1 - row)

    root = (grp, 0, row)

    def own_copy(k):
        return pltpu.make_async_copy(calls_hbm.at[k], own.at[k], local_sem.at[k])

    for k in range(blocks):
        own_copy(k).start()

    barrier = pltpu.get_barrier_semaphore()
    pl.semaphore_signal(barrier, inc=1, device_id=pair, device_id_type=MESH)

    @pl.when(jnp.logical_not(is_root))
    def _():
        pl.semaphore_signal(barrier, inc=1, device_id=parent, device_id_type=MESH)

    @pl.when(is_root)
    def _():
        def greet(j, carry):
            pl.semaphore_signal(barrier, inc=1, device_id=(grp, j, row), device_id_type=MESH)
            return carry

        lax.fori_loop(1, columns, greet, 0)

    pl.semaphore_wait(
        barrier,
        1 + jnp.where(is_root, 0, 1) + jnp.where(has_a, 1, 0) + jnp.where(has_b, 1, 0))

    def place_of(c):
        if isinstance(c, tuple):
            return c
        return lax.div(c, PIECES), lax.rem(c, PIECES)

    def index_of(c):
        return c[0] * PIECES + c[1] if isinstance(c, tuple) else c

    def part(ref, c):
        k, j = place_of(c)
        return ref.at[k, pl.ds(pl.multiple_of(j * piece, piece), piece)]

    def from_root(c):
        return pltpu.make_async_remote_copy(
            src_ref=part(calls_hbm, c), dst_ref=part(rows, c), send_sem=root_send.at[index_of(c)],
            recv_sem=piece_recv.at[index_of(c)], device_id=child_a, device_id_type=MESH)

    def forward(c, which, target):
        return pltpu.make_async_remote_copy(
            src_ref=part(rows, c), dst_ref=part(rows, c), send_sem=piece_send.at[which],
            recv_sem=piece_recv.at[index_of(c)], device_id=target, device_id_type=MESH)

    def pair_copy(k):
        return pltpu.make_async_remote_copy(
            src_ref=calls_hbm.at[k], dst_ref=other.at[k], send_sem=pair_send,
            recv_sem=pair_recv.at[k], device_id=pair, device_id_type=MESH)

    def sums_copy(j):
        return pltpu.make_async_remote_copy(
            src_ref=sums, dst_ref=gathered.at[j], send_sem=sums_send, recv_sem=sums_recv.at[j],
            device_id=root, device_id_type=MESH)

    joined_copy = pltpu.make_async_remote_copy(
        src_ref=joined, dst_ref=joined_in, send_sem=joined_sem.at[0], recv_sem=joined_sem.at[1],
        device_id=pair, device_id_type=MESH)

    def totals_copy(which, target):
        return pltpu.make_async_remote_copy(
            src_ref=totals, dst_ref=totals, send_sem=totals_send.at[which], recv_sem=totals_recv,
            device_id=target, device_id_type=MESH)

    @pl.when(is_root)
    def _():
        for j in range(PIECES):
            from_root((0, j)).start()

    def local_sums(k, carry):
        own_copy(k).wait()
        values = own[k]
        called = values >= 0
        dosage = jnp.where(called, values, 0.0)
        sums[0, pl.ds(k, 1), :] = jnp.sum(dosage, axis=0, keepdims=True)
        sums[1, pl.ds(k, 1), :] = jnp.sum(dosage * dosage, axis=0, keepdims=True)
        sums[2, pl.ds(k, 1), :] = jnp.sum(jnp.where(called, 1.0, 0.0), axis=0, keepdims=True)
        return carry

    lax.fori_loop(0, blocks, local_sums, 0)

    @pl.when(jnp.logical_not(is_root))
    def _():
        sums_copy(col).start()

    out_ref[...] = jnp.zeros_like(out_ref)
    factor = 1.0 / math.sqrt(blocks * variants)

    def standardize(values, k):
        center, scale = scaling[0, pl.ds(k, 1), :], scaling[1, pl.ds(k, 1), :]
        return jnp.where(values >= 0, (values - center) * scale, 0.0)

    def prepare_column(k):
        for held, place in ((own, row), (other, 1 - row)):
            first_part, second_part = split(standardize(held[k], k) * factor)
            spot = pl.ds(pl.multiple_of(place * samples, samples), samples)
            high[k, spot, :] = first_part
            low[k, spot, :] = second_part

    def prepare_row(c):
        k, j = place_of(c)
        spot = pl.ds(pl.multiple_of(j * piece, piece), piece)

        def prepare(held):
            first_part, second_part = split(standardize(held[k, spot, :], k))
            row_high[k, spot, :] = first_part
            row_low[k, spot, :] = second_part

        @pl.when(is_root)
        def _():
            prepare(own)

        @pl.when(jnp.logical_not(is_root))
        def _():
            prepare(rows)

    def product(left, right):
        return lax.dot_general(
            left, right, (((1,), (1,)), ((), ())), preferred_element_type=jnp.float32)

    def multiply(k, begin, end, top=0, bottom=samples):
        left_high, left_low = row_high[k, top:bottom, :], row_low[k, top:bottom, :]
        right_high, right_low = high[k, begin:end, :], low[k, begin:end, :]
        out_ref[top:bottom, begin:end] += (
            product(left_high, right_high)
            + (product(left_low, right_high) + product(left_high, right_low)))

    width = out_ref.shape[1]

    def step(k, j):
        c = k * PIECES + j
        now = (k, j)

        @pl.when(jnp.logical_not(is_root))
        def _():
            forward(now, 0, parent).wait_recv()

            @pl.when(has_a)
            def _():
                forward(now, 0, child_a).start()

            @pl.when(has_b)
            def _():
                forward(now, 1, child_b).start()

            @pl.when(c == arrival)
            def _():
                totals_copy(0, parent).wait_recv()

                @pl.when(has_a)
                def _():
                    totals_copy(0, child_a).start()

                @pl.when(has_b)
                def _():
                    totals_copy(1, child_b).start()

        @pl.when(is_root)
        def _():
            from_root(now).wait_send()

            @pl.when(k + 1 < blocks)
            def _():
                from_root((k + 1, j)).start()

            @pl.when(c == GATHERED)
            def _():
                joined[...] = sums[...]

                def add(j, carry):
                    sums_copy(j).wait_recv()
                    joined[...] += gathered[j]
                    return carry

                lax.fori_loop(1, columns, add, 0)
                joined_copy.start()

            @pl.when(c == TOTALLED)
            def _():
                joined_copy.wait_recv()
                totals[...] = joined[...] + joined_in[...]
                totals_copy(0, child_a).start()

        @pl.when(c == arrival)
        def _():
            counts = jnp.maximum(totals[2], 1.0)
            center = totals[0] / counts
            spread = jnp.sqrt(jnp.maximum(totals[1] / counts - center * center, 0.05))
            scaling[0] = center
            scaling[1] = 1.0 / spread

        @pl.when(jnp.logical_and(c >= 1, c < 1 + blocks))
        def _():
            pair_copy(c - 1).start()

        since = c - arrival - 1

        @pl.when(jnp.logical_and(since >= 0, since < blocks))
        def _():
            pair_copy(since).wait_recv()
            prepare_column(since)

        for j in range(2):
            @pl.when(jnp.logical_and(since >= 0, 2 * since + j <= c))
            def _():
                prepare_row(2 * since + j)

        @pl.when(jnp.logical_and(since >= 0, c < 2 * since))
        def _():
            prepare_row(now)

        late = arrival + PIECES // 2 + LATE
        steps = [max(late + b * (PIECES // 2), (b + 1) * PIECES - 1) for b in range(blocks - 1)]
        for half in range(2):
            chosen = [c == at + half for at in steps]

            @pl.when(functools.reduce(jnp.logical_or, chosen))
            def _():
                b = sum(jnp.where(is_now, b, 0) for b, is_now in enumerate(chosen))
                multiply(b, half * width // 2, (half + 1) * width // 2)

        @pl.when(c == pieces - PIECES // 2)
        def _():
            multiply(blocks - 1, 0, width, 0, samples // 2)

    def block_steps(k, carry):
        def one(j, carry):
            step(k, j)
            return carry

        return lax.fori_loop(0, PIECES, one, carry)

    lax.fori_loop(0, blocks, block_steps, 0)
    multiply(blocks - 1, 0, width, samples // 2, samples)

    @pl.when(is_root)
    def _():
        joined_copy.wait_send()
        totals_copy(0, child_a).wait_send()

    @pl.when(jnp.logical_not(is_root))
    def _():
        sums_copy(col).wait_send()

        @pl.when(has_a)
        def _():
            totals_copy(0, child_a).wait_send()

        @pl.when(has_b)
        def _():
            totals_copy(1, child_b).wait_send()

    def all_sent(which, target):
        return pltpu.make_async_remote_copy(
            src_ref=rows, dst_ref=rows, send_sem=piece_send.at[which],
            recv_sem=piece_recv.at[0], device_id=target, device_id_type=MESH)

    pltpu.make_async_remote_copy(
        src_ref=own, dst_ref=other, send_sem=pair_send, recv_sem=pair_recv.at[0],
        device_id=pair, device_id_type=MESH).wait_send()

    @pl.when(jnp.logical_and(has_a, jnp.logical_not(is_root)))
    def _():
        all_sent(0, child_a).wait_send()

    @pl.when(has_b)
    def _():
        all_sent(1, child_b).wait_send()


def per_device(slow_n, fast_n, genotypes, prior_slab):
    blocks, samples, variants = genotypes.shape
    height, width = prior_slab.shape
    columns = slow_n * fast_n
    pieces = blocks * PIECES
    calls = pltpu.VMEM((blocks, samples, variants), jnp.float32)
    column_part = pltpu.VMEM((blocks, width, variants), jnp.bfloat16)
    row_part = pltpu.VMEM((blocks, samples, variants), jnp.bfloat16)
    sums = pltpu.VMEM((3, blocks, variants), jnp.float32)
    accumulated = pl.pallas_call(
        functools.partial(kernel, slow_n, fast_n),
        out_shape=jax.ShapeDtypeStruct((height, width), jnp.float32),
        in_specs=[pl.BlockSpec(memory_space=pl.ANY)],
        out_specs=pl.BlockSpec(memory_space=pltpu.VMEM),
        scratch_shapes=[
            calls, calls, calls, column_part, column_part, row_part, row_part,
            sums, pltpu.VMEM((columns, 3, blocks, variants), jnp.float32), sums, sums, sums,
            pltpu.VMEM((2, blocks, variants), jnp.float32),
            pltpu.SemaphoreType.DMA((blocks,)),
            pltpu.SemaphoreType.DMA,
            pltpu.SemaphoreType.DMA((blocks,)),
            pltpu.SemaphoreType.DMA,
            pltpu.SemaphoreType.DMA((columns,)),
            pltpu.SemaphoreType.DMA((2,)),
            pltpu.SemaphoreType.DMA((2,)),
            pltpu.SemaphoreType.DMA,
            pltpu.SemaphoreType.DMA((pieces,)),
            pltpu.SemaphoreType.DMA((2,)),
            pltpu.SemaphoreType.DMA((pieces,)),
        ],
        compiler_params=pltpu.CompilerParams(
            collective_id=0, has_side_effects=True, vmem_limit_bytes=VMEM_MIB * 2**20),
        cost_estimate=pl.CostEstimate(
            flops=6 * height * width * blocks * variants,
            bytes_accessed=4 * (blocks * samples * variants + height * width),
            transcendentals=0),
    )(genotypes)
    return prior_slab + accumulated


def solution(mesh):
    slow_n, fast_n = grid_of(mesh.shape["col"])
    placed = (P(None, ("grp", "col", "row"), None), P(("grp", "row"), "col"))
    return jax.shard_map(
        functools.partial(per_device, slow_n, fast_n), mesh=mesh, in_specs=placed,
        out_specs=P(("grp", "row"), "col"), check_vma=False
    )
```

```python
import functools
import math

import jax
import jax.numpy as jnp
from jax import lax
from jax.experimental import pallas as pl
from jax.experimental.pallas import tpu as pltpu
from jax.sharding import PartitionSpec as P

MESH = pl.DeviceIdType.MESH
PIECES = 8
LATE = 3
GATHERED = 6
TOTALLED = 9
VMEM_MIB = 52


def grid_of(count):
    fast = 2 ** (int(math.log2(count)) // 2)
    return count // fast, fast


def split(values):
    high = values.astype(jnp.bfloat16)
    return high, (values - high.astype(jnp.float32)).astype(jnp.bfloat16)


def kernel(slow_n, fast_n, calls_hbm, out_ref, own, other, rows, high, low, row_high, row_low,
           sums, gathered, joined, joined_in, totals, scaling, local_sem, pair_send, pair_recv,
           sums_send, sums_recv, joined_sem, totals_send, totals_recv, root_send,
           piece_send, piece_recv):
    blocks, samples, variants = own.shape
    columns = gathered.shape[0]
    piece = samples // PIECES
    pieces = blocks * PIECES
    arrival = TOTALLED + PIECES

    grp, col, row = lax.axis_index("grp"), lax.axis_index("col"), lax.axis_index("row")
    z, x = lax.div(col, fast_n), lax.rem(col, fast_n)
    first, second = jnp.where(row == 0, z, x), jnp.where(row == 0, x, z)
    first_n = jnp.where(row == 0, slow_n, fast_n)
    second_n = jnp.where(row == 0, fast_n, slow_n)

    def device(a, b):
        return (grp, jnp.where(row == 0, a * fast_n + b, b * fast_n + a), row)

    is_root = col == 0
    on_edge = jnp.logical_and(first == 0, second > 0)
    on_spine = second == 0
    on_line = jnp.logical_and(first > 0, second > 0)
    skips = second_n >= 3
    before = jnp.where(jnp.logical_and(skips, second == 1), 2,
                       jnp.where(jnp.logical_and(skips, second == 2), 0, second - 1))
    parent = device(
        jnp.where(on_edge, 1, jnp.where(on_spine, jnp.maximum(first - 1, 0), first)),
        jnp.where(on_edge, second, jnp.where(on_spine, 0, before)),
    )
    has_a = jnp.logical_and(
        jnp.logical_not(on_edge),
        jnp.where(on_spine, first + 1 < first_n,
                  jnp.logical_and(second + 1 < second_n,
                                  jnp.logical_not(jnp.logical_and(skips, second == 1)))),
    )
    child_a = device(
        jnp.where(on_spine, jnp.minimum(first + 1, first_n - 1), first),
        jnp.where(on_spine, 0, jnp.minimum(second + 1, second_n - 1)),
    )
    has_b = jnp.where(on_spine, first >= 1, first == 1)
    child_b = device(
        jnp.where(on_spine, first, 0),
        jnp.where(on_spine, jnp.where(skips, 2, 1), second))
    has_c = jnp.logical_and(jnp.logical_and(skips, on_line), second == 2)
    child_c = device(first, jnp.minimum(1, second_n - 1))

    pair = (grp, col, 1 - row)

    root = (grp, 0, row)

    def own_copy(k):
        return pltpu.make_async_copy(calls_hbm.at[k], own.at[k], local_sem.at[k])

    for k in range(blocks):
        own_copy(k).start()

    barrier = pltpu.get_barrier_semaphore()
    pl.semaphore_signal(barrier, inc=1, device_id=pair, device_id_type=MESH)

    @pl.when(jnp.logical_not(is_root))
    def _():
        pl.semaphore_signal(barrier, inc=1, device_id=parent, device_id_type=MESH)

    @pl.when(is_root)
    def _():
        def greet(j, carry):
            pl.semaphore_signal(barrier, inc=1, device_id=(grp, j, row), device_id_type=MESH)
            return carry

        lax.fori_loop(1, columns, greet, 0)

    pl.semaphore_wait(
        barrier,
        1 + jnp.where(is_root, 0, 1) + jnp.where(has_a, 1, 0) + jnp.where(has_b, 1, 0)
        + jnp.where(has_c, 1, 0))

    def place_of(c):
        if isinstance(c, tuple):
            return c
        return lax.div(c, PIECES), lax.rem(c, PIECES)

    def index_of(c):
        return c[0] * PIECES + c[1] if isinstance(c, tuple) else c

    def part(ref, c):
        k, j = place_of(c)
        return ref.at[k, pl.ds(pl.multiple_of(j * piece, piece), piece)]

    def from_root(c):
        return pltpu.make_async_remote_copy(
            src_ref=part(calls_hbm, c), dst_ref=part(rows, c), send_sem=root_send.at[index_of(c)],
            recv_sem=piece_recv.at[index_of(c)], device_id=child_a, device_id_type=MESH)

    def forward(c, which, target):
        return pltpu.make_async_remote_copy(
            src_ref=part(rows, c), dst_ref=part(rows, c), send_sem=piece_send.at[which],
            recv_sem=piece_recv.at[index_of(c)], device_id=target, device_id_type=MESH)

    def pair_copy(k):
        return pltpu.make_async_remote_copy(
            src_ref=calls_hbm.at[k], dst_ref=other.at[k], send_sem=pair_send,
            recv_sem=pair_recv.at[k], device_id=pair, device_id_type=MESH)

    def sums_copy(j):
        return pltpu.make_async_remote_copy(
            src_ref=sums, dst_ref=gathered.at[j], send_sem=sums_send, recv_sem=sums_recv.at[j],
            device_id=root, device_id_type=MESH)

    joined_copy = pltpu.make_async_remote_copy(
        src_ref=joined, dst_ref=joined_in, send_sem=joined_sem.at[0], recv_sem=joined_sem.at[1],
        device_id=pair, device_id_type=MESH)

    def totals_copy(which, target):
        return pltpu.make_async_remote_copy(
            src_ref=totals, dst_ref=totals, send_sem=totals_send.at[which], recv_sem=totals_recv,
            device_id=target, device_id_type=MESH)

    @pl.when(is_root)
    def _():
        for j in range(PIECES):
            from_root((0, j)).start()

    def local_sums(k, carry):
        own_copy(k).wait()
        values = own[k]
        called = values >= 0
        dosage = jnp.where(called, values, 0.0)
        sums[0, pl.ds(k, 1), :] = jnp.sum(dosage, axis=0, keepdims=True)
        sums[1, pl.ds(k, 1), :] = jnp.sum(dosage * dosage, axis=0, keepdims=True)
        sums[2, pl.ds(k, 1), :] = jnp.sum(jnp.where(called, 1.0, 0.0), axis=0, keepdims=True)
        return carry

    lax.fori_loop(0, blocks, local_sums, 0)

    @pl.when(jnp.logical_not(is_root))
    def _():
        sums_copy(col).start()

    out_ref[...] = jnp.zeros_like(out_ref)
    factor = 1.0 / math.sqrt(blocks * variants)

    def standardize(values, k):
        center, scale = scaling[0, pl.ds(k, 1), :], scaling[1, pl.ds(k, 1), :]
        return jnp.where(values >= 0, (values - center) * scale, 0.0)

    def prepare_column(k):
        for held, place in ((own, row), (other, 1 - row)):
            first_part, second_part = split(standardize(held[k], k) * factor)
            spot = pl.ds(pl.multiple_of(place * samples, samples), samples)
            high[k, spot, :] = first_part
            low[k, spot, :] = second_part

    def prepare_row(c):
        k, j = place_of(c)
        spot = pl.ds(pl.multiple_of(j * piece, piece), piece)

        def prepare(held):
            first_part, second_part = split(standardize(held[k, spot, :], k))
            row_high[k, spot, :] = first_part
            row_low[k, spot, :] = second_part

        @pl.when(is_root)
        def _():
            prepare(own)

        @pl.when(jnp.logical_not(is_root))
        def _():
            prepare(rows)

    def product(left, right):
        return lax.dot_general(
            left, right, (((1,), (1,)), ((), ())), preferred_element_type=jnp.float32)

    def multiply(k, begin, end, top=0, bottom=samples):
        left_high, left_low = row_high[k, top:bottom, :], row_low[k, top:bottom, :]
        right_high, right_low = high[k, begin:end, :], low[k, begin:end, :]
        out_ref[top:bottom, begin:end] += (
            product(left_high, right_high)
            + (product(left_low, right_high) + product(left_high, right_low)))

    width = out_ref.shape[1]

    def step(k, j):
        c = k * PIECES + j
        now = (k, j)

        @pl.when(jnp.logical_not(is_root))
        def _():
            forward(now, 0, parent).wait_recv()

            @pl.when(has_a)
            def _():
                forward(now, 0, child_a).start()

            @pl.when(has_c)
            def _():
                forward(now, 2, child_c).start()

            @pl.when(has_b)
            def _():
                forward(now, 1, child_b).start()

            @pl.when(c == arrival)
            def _():
                totals_copy(0, parent).wait_recv()

                @pl.when(has_a)
                def _():
                    totals_copy(0, child_a).start()

                @pl.when(has_b)
                def _():
                    totals_copy(1, child_b).start()

                @pl.when(has_c)
                def _():
                    totals_copy(2, child_c).start()

        @pl.when(is_root)
        def _():
            from_root(now).wait_send()

            @pl.when(k + 1 < blocks)
            def _():
                from_root((k + 1, j)).start()

            @pl.when(c == GATHERED)
            def _():
                joined[...] = sums[...]

                def add(j, carry):
                    sums_copy(j).wait_recv()
                    joined[...] += gathered[j]
                    return carry

                lax.fori_loop(1, columns, add, 0)
                joined_copy.start()

            @pl.when(c == TOTALLED)
            def _():
                joined_copy.wait_recv()
                totals[...] = joined[...] + joined_in[...]
                totals_copy(0, child_a).start()

        @pl.when(c == arrival)
        def _():
            counts = jnp.maximum(totals[2], 1.0)
            center = totals[0] / counts
            spread = jnp.sqrt(jnp.maximum(totals[1] / counts - center * center, 0.05))
            scaling[0] = center
            scaling[1] = 1.0 / spread

        @pl.when(jnp.logical_and(c >= 1, c < 1 + blocks))
        def _():
            pair_copy(c - 1).start()

        since = c - arrival - 1

        @pl.when(jnp.logical_and(since >= 0, since < blocks))
        def _():
            pair_copy(since).wait_recv()
            prepare_column(since)

        for j in range(2):
            @pl.when(jnp.logical_and(since >= 0, 2 * since + j <= c))
            def _():
                prepare_row(2 * since + j)

        @pl.when(jnp.logical_and(since >= 0, c < 2 * since))
        def _():
            prepare_row(now)

        late = arrival + PIECES // 2 + LATE
        steps = [max(late + b * (PIECES // 2), (b + 1) * PIECES - 1) for b in range(blocks - 1)]
        for half in range(2):
            chosen = [c == at + half for at in steps]

            @pl.when(functools.reduce(jnp.logical_or, chosen))
            def _():
                b = sum(jnp.where(is_now, b, 0) for b, is_now in enumerate(chosen))
                multiply(b, half * width // 2, (half + 1) * width // 2)

        @pl.when(c == pieces - PIECES // 2)
        def _():
            multiply(blocks - 1, 0, width, 0, samples // 2)

    def block_steps(k, carry):
        def one(j, carry):
            step(k, j)
            return carry

        return lax.fori_loop(0, PIECES, one, carry)

    lax.fori_loop(0, blocks, block_steps, 0)
    multiply(blocks - 1, 0, width, samples // 2, samples)

    @pl.when(is_root)
    def _():
        joined_copy.wait_send()
        totals_copy(0, child_a).wait_send()

    @pl.when(jnp.logical_not(is_root))
    def _():
        sums_copy(col).wait_send()

        @pl.when(has_a)
        def _():
            totals_copy(0, child_a).wait_send()

        @pl.when(has_b)
        def _():
            totals_copy(1, child_b).wait_send()

        @pl.when(has_c)
        def _():
            totals_copy(2, child_c).wait_send()

    def all_sent(which, target):
        return pltpu.make_async_remote_copy(
            src_ref=rows, dst_ref=rows, send_sem=piece_send.at[which],
            recv_sem=piece_recv.at[0], device_id=target, device_id_type=MESH)

    pltpu.make_async_remote_copy(
        src_ref=own, dst_ref=other, send_sem=pair_send, recv_sem=pair_recv.at[0],
        device_id=pair, device_id_type=MESH).wait_send()

    @pl.when(jnp.logical_and(has_a, jnp.logical_not(is_root)))
    def _():
        all_sent(0, child_a).wait_send()

    @pl.when(has_b)
    def _():
        all_sent(1, child_b).wait_send()

    @pl.when(has_c)
    def _():
        all_sent(2, child_c).wait_send()


def per_device(slow_n, fast_n, genotypes, prior_slab):
    blocks, samples, variants = genotypes.shape
    height, width = prior_slab.shape
    columns = slow_n * fast_n
    pieces = blocks * PIECES
    calls = pltpu.VMEM((blocks, samples, variants), jnp.float32)
    column_part = pltpu.VMEM((blocks, width, variants), jnp.bfloat16)
    row_part = pltpu.VMEM((blocks, samples, variants), jnp.bfloat16)
    sums = pltpu.VMEM((3, blocks, variants), jnp.float32)
    accumulated = pl.pallas_call(
        functools.partial(kernel, slow_n, fast_n),
        out_shape=jax.ShapeDtypeStruct((height, width), jnp.float32),
        in_specs=[pl.BlockSpec(memory_space=pl.ANY)],
        out_specs=pl.BlockSpec(memory_space=pltpu.VMEM),
        scratch_shapes=[
            calls, calls, calls, column_part, column_part, row_part, row_part,
            sums, pltpu.VMEM((columns, 3, blocks, variants), jnp.float32), sums, sums, sums,
            pltpu.VMEM((2, blocks, variants), jnp.float32),
            pltpu.SemaphoreType.DMA((blocks,)),
            pltpu.SemaphoreType.DMA,
            pltpu.SemaphoreType.DMA((blocks,)),
            pltpu.SemaphoreType.DMA,
            pltpu.SemaphoreType.DMA((columns,)),
            pltpu.SemaphoreType.DMA((2,)),
            pltpu.SemaphoreType.DMA((3,)),
            pltpu.SemaphoreType.DMA,
            pltpu.SemaphoreType.DMA((pieces,)),
            pltpu.SemaphoreType.DMA((3,)),
            pltpu.SemaphoreType.DMA((pieces,)),
        ],
        compiler_params=pltpu.CompilerParams(
            collective_id=0, has_side_effects=True, vmem_limit_bytes=VMEM_MIB * 2**20),
        cost_estimate=pl.CostEstimate(
            flops=6 * height * width * blocks * variants,
            bytes_accessed=4 * (blocks * samples * variants + height * width),
            transcendentals=0),
    )(genotypes)
    return prior_slab + accumulated


def solution(mesh):
    slow_n, fast_n = grid_of(mesh.shape["col"])
    placed = (P(None, ("grp", "col", "row"), None), P(("grp", "row"), "col"))
    return jax.shard_map(
        functools.partial(per_device, slow_n, fast_n), mesh=mesh, in_specs=placed,
        out_specs=P(("grp", "row"), "col"), check_vma=False
    )
```
